32 devices in a mesh: recv: 8 (over z, y), tm: 4 (over x, core).
Axes of the slice: x: 2, y: 2, z: 4, core: 2. Of those that a mesh axis runs over, the one named last changes fastest.
Arguments:
- spectra: bfloat16 [2, 128, 64, 512], P(None, 'tm', 'recv'), may hold values from -6 to 6
- owners: int32 [4], replicated, may hold values from 0 to 7
- source_slots: int32 [4, 8], replicated, may hold values from 0 to 7, as said below
Outputs:
- correlations: float32 [32, 64, 512], P('tm', 'recv')
The draws below stay inside these ranges and needn't reach their ends.
Inputs may be any that keep to these rules, and one draw needn't show every extreme that they name: Block k of sources lies among the channels of recv index owners[k]. `source_slots`: the 8 slots of one block are distinct.
All inputs are finite; a program needn't handle non-finite values.
Results may differ from the reference program's by a relative error of at most 0.0019.
Values may be sent and summed in bfloat16 or wider, within the bound.
A program may use at most 64 MiB of HBM per device.

```python
import jax
import jax.numpy as jnp
from jax import lax

F = 512
HALF = 64
RECV_DEV = 8
STEPS = 4
SB = 8
SOURCES = 32
WINDOWS = 128
RECEIVERS = 64
N_RECV = 8


def draw_source_slots(key, part):
    key = jax.random.fold_in(key, 7)
    step_keys = jax.random.split(key, STEPS)
    chosen = jax.vmap(lambda one_key: jax.random.permutation(one_key, RECV_DEV)[:SB])(step_keys)
    return chosen.astype(jnp.int32)


def touch_ends(drawn, stream_key, smallest, largest):
    dims = drawn.shape
    spot = [jax.random.randint(jax.random.fold_in(stream_key, axis), (), 0, dims[axis]) for axis in range(len(dims))]
    drawn = drawn.at[tuple(spot)].set(smallest)
    longest = dims.index(max(dims))
    spot[longest] = (spot[longest] + 1) % dims[longest]
    return drawn.at[tuple(spot)].set(largest)


def block_scale(key, dims, pieces, least, top_value):
    def one(dim, shards_of):
        steps = jax.random.uniform(jax.random.fold_in(jax.random.fold_in(key, 6), dim), (shards_of,), jnp.float32, least / len(pieces), top_value / len(pieces))
        return jnp.repeat(jnp.exp(steps), dims[dim] // shards_of).reshape((-1,) + (1,) * (len(dims) - dim - 1))

    loudness = one(*pieces[0])
    for cut in pieces[1:]:
        loudness = loudness * one(*cut)
    return loudness


def scatter_about(rng, extent, scale, reach, cuts=(), dtype=jnp.bfloat16):
    level = block_scale(rng, extent, cuts, -0.22, 0.18) if cuts else 1.0
    array = jax.random.normal(rng, extent, jnp.float32) * scale * level
    return jnp.minimum(jnp.maximum(array, -reach), reach).astype(dtype)


def setup_inputs(seed: int = 0) -> dict:
    key_of = jax.random.split(jax.random.key(seed), 4)
    return {
        "spectra": scatter_about(key_of[0], (2, WINDOWS, RECEIVERS, F), 1.0, 6.0, ((1, 4), (2, 8))),
        "owners": touch_ends(jax.random.randint(key_of[1], (STEPS,), 0, N_RECV), jax.random.fold_in(key_of[1], 1), 0, N_RECV - 1).astype(jnp.int32),
        "source_slots": draw_source_slots(jax.random.fold_in(key_of[3], 71), 0),
    }


epsilon = 1e-05

def band_matrix():
    positions = jnp.arange(F)
    near = (jnp.abs(positions[:, None] - positions[None, :]) <= HALF).astype(jnp.float32)
    return near / lax.optimization_barrier(jnp.sum(near, axis=0, keepdims=True))

def whiten(block, band_table):
    parts = block.astype(jnp.float32)
    energy = parts[0] * parts[0] + parts[1] * parts[1]
    smooth = jnp.matmul(energy, band_table, precision=lax.Precision.HIGHEST)
    return (parts * lax.rsqrt(smooth + epsilon)[None]).astype(jnp.bfloat16)

def reference(spectra, owners, source_slots):
    band_table = band_matrix()
    channel = (owners[:, None] * RECV_DEV + source_slots).reshape(-1).astype(jnp.int32)
    source = whiten(jnp.take(spectra, channel, axis=2), band_table).astype(jnp.float32)
    high = lax.Precision.HIGHEST

    def one_block(number):
        block = lax.dynamic_slice_in_dim(spectra, number * RECV_DEV, RECV_DEV, 2)
        whitened = whiten(block, band_table).astype(jnp.float32)
        cross_real = jnp.einsum('wsf,wrf->srf', source[0], whitened[0], precision=high) + jnp.einsum('wsf,wrf->srf', source[1], whitened[1], precision=high)
        cross_imag = jnp.einsum('wsf,wrf->srf', source[0], whitened[1], precision=high) - jnp.einsum('wsf,wrf->srf', source[1], whitened[0], precision=high)
        return jnp.real(jnp.fft.ifft(cross_real + 1j * cross_imag, axis=-1)).astype(jnp.float32)
    lag_blocks = lax.map(one_block, jnp.arange(N_RECV))
    return jnp.transpose(lag_blocks, (1, 0, 2, 3)).reshape(SOURCES, RECEIVERS, F)
```

```python
import math

import jax
import jax.numpy as jnp
import numpy as np
from jax import lax
from jax.experimental import pallas as pl
from jax.experimental.pallas import tpu as pltpu
from jax.sharding import PartitionSpec as P

HALF = 64
STEPS = 4
BINS = 16
PAIRS = BINS // 2

epsilon = 1e-05
MESH = pl.DeviceIdType.MESH
NT = (((1,), (1,)), ((), ()))


def broadcast(value, axis, source):
    kept = jnp.where(lax.axis_index(axis) == source, value, 0).astype(value.dtype)
    return lax.psum(kept, axis)


def band_matrix(length, half_width):
    positions = lax.iota(jnp.int32, length)
    near = (jnp.abs(positions[:, None] - positions[None, :]) <= half_width).astype(jnp.float32)
    return near / jnp.sum(near, axis=0, keepdims=True)


def transform_tables(length):
    positions = lax.iota(jnp.int32, length)
    phase = positions[:, None] * positions[None, :] % length
    angle = phase.astype(jnp.float32) * (2.0 * math.pi / length)
    return (jnp.cos(angle), jnp.sin(angle))


def inverse_lags(cross_real, cross_imag, cosine, sine):
    length = cross_real.shape[-1]
    high = lax.Precision.HIGHEST
    flat_real = cross_real.reshape(-1, length)
    flat_imag = cross_imag.reshape(-1, length)
    lag_terms = jnp.dot(
        flat_real, cosine, precision=high, preferred_element_type=jnp.float32
    ) - jnp.dot(flat_imag, sine, precision=high, preferred_element_type=jnp.float32)
    return (lag_terms / length).reshape(cross_real.shape)


def per_device_gathered(spectra, owners, source_slots):
    length = spectra.shape[3]
    width = spectra.shape[2]
    band_table = band_matrix(length, HALF)
    parts = spectra.astype(jnp.float32)
    energy = parts[0] * parts[0] + parts[1] * parts[1]
    smooth = jnp.dot(
        energy.reshape(-1, length),
        band_table,
        precision=lax.Precision.HIGHEST,
        preferred_element_type=jnp.float32,
    ).reshape(energy.shape)
    whitened = (parts * lax.rsqrt(smooth + epsilon)[None]).astype(jnp.bfloat16)
    positions = lax.iota(jnp.int32, width)
    real_parts = []
    imag_parts = []
    for step in range(STEPS):
        selector = (source_slots[step][:, None] == positions[None, :]).astype(jnp.bfloat16)
        picked = jnp.einsum(
            "sr,cwrf->cwsf", selector, whitened, preferred_element_type=jnp.float32
        ).astype(jnp.bfloat16)
        arrived = broadcast(picked, "recv", owners[step])
        real_parts.append(
            jnp.einsum("wsf,wrf->srf", arrived[0], whitened[0], preferred_element_type=jnp.float32)
            + jnp.einsum(
                "wsf,wrf->srf", arrived[1], whitened[1], preferred_element_type=jnp.float32
            )
        )
        imag_parts.append(
            jnp.einsum("wsf,wrf->srf", arrived[0], whitened[1], preferred_element_type=jnp.float32)
            - jnp.einsum(
                "wsf,wrf->srf", arrived[1], whitened[0], preferred_element_type=jnp.float32
            )
        )
    cross_real = jnp.concatenate(real_parts, axis=0)
    cross_imag = jnp.concatenate(imag_parts, axis=0)
    cosine, sine = transform_tables(length)
    return lax.psum_scatter(
        inverse_lags(cross_real, cross_imag, cosine, sine), "tm", scatter_dimension=0, tiled=True
    )


def constant_tables(length):
    low = np.arange(length // 2)
    mirror = np.where(low == 0, length // 2, length - low)
    order = np.stack([low.reshape(-1, PAIRS), mirror.reshape(-1, PAIRS)], axis=1).reshape(-1)
    places = np.arange(length)
    regroup = (order[:, None] == places[None, :]).astype(np.float32)
    near = (np.abs(places[:, None] - places[None, :]) <= HALF).astype(np.float32)
    share = 1.0 / near.sum(axis=0, keepdims=True)
    angle = (low[:, None] * places[None, :] % length) * (2.0 * math.pi / length)
    cosine = np.cos(angle) / length
    sine = -np.sin(angle) / length
    sine[0] = np.where(places % 2 == 0, 1.0, -1.0) / length
    table = np.concatenate([cosine, sine], axis=0).astype(np.float32)
    high = table.astype(jnp.bfloat16)
    rest = (table - high.astype(np.float32)).astype(jnp.bfloat16)
    return (
        regroup.astype(jnp.bfloat16),
        near.astype(jnp.bfloat16),
        share.astype(np.float32),
        high,
        rest,
    )


def split(value):
    high = value.astype(jnp.bfloat16)
    return high, (value - high.astype(jnp.float32)).astype(jnp.bfloat16)


def dot(a, b):
    return jnp.dot(a, b, preferred_element_type=jnp.float32)


def kernel(
    n_recv, n_tm, windows, width, length,
    x_ref, owners_ref, slots_ref, regroup_ref, near_ref, share_ref, high_ref, rest_ref,
    out_ref,
    outgoing, arrived, plain, sources, cross, folded, landed,
    send_sem, recv_sem, send2_sem, recv2_sem,
):
    f32, bf16 = jnp.float32, jnp.bfloat16
    devices = n_recv * n_tm
    rows = windows * width
    lanes = n_recv * BINS
    my_recv, my_tm = lax.axis_index("recv"), lax.axis_index("tm")
    me = my_recv * n_tm + my_tm

    def partner(step, sign):
        other_recv = lax.rem(my_recv + sign * lax.rem(step, n_recv) + n_recv, n_recv)
        other_tm = lax.rem(my_tm + sign * (step // n_recv) + n_tm, n_tm)
        return other_recv, other_tm

    barrier = pltpu.get_barrier_semaphore()

    def greet(step, carry):
        other_recv, other_tm = partner(step, 1)
        pl.semaphore_signal(
            barrier, inc=1, device_id={"recv": other_recv, "tm": other_tm}, device_id_type=MESH
        )
        return carry

    lax.fori_loop(1, devices, greet, 0)

    real = x_ref[0].astype(f32).reshape(rows, length)
    imag = x_ref[1].astype(f32).reshape(rows, length)
    energy_high, energy_rest = split(real * real + imag * imag)
    near = near_ref[...]
    smooth = (dot(energy_high, near) + dot(energy_rest, near)) * share_ref[...]
    gain = lax.rsqrt(smooth + epsilon)
    regroup = regroup_ref[...]
    for part, value in enumerate((real, imag)):
        white = (value * gain).astype(bf16)
        outgoing[:, part * rows : (part + 1) * rows] = lax.dot_general(
            regroup, white, NT, preferred_element_type=f32
        ).astype(bf16)

    def bins_of(device):
        return pl.ds(pl.multiple_of(device * BINS, BINS), BINS)

    def first_copy(step):
        other_recv, other_tm = partner(step, 1)
        return pltpu.make_async_remote_copy(
            src_ref=outgoing.at[bins_of(other_recv * n_tm + other_tm)],
            dst_ref=arrived.at[my_tm, bins_of(my_recv)],
            send_sem=send_sem.at[step],
            recv_sem=recv_sem.at[step],
            device_id={"recv": other_recv, "tm": other_tm},
            device_id_type=MESH,
        )

    def first_arrival(step):
        other_recv, other_tm = partner(step, -1)
        return pltpu.make_async_remote_copy(
            src_ref=outgoing.at[bins_of(other_recv * n_tm + other_tm)],
            dst_ref=arrived.at[other_tm, bins_of(other_recv)],
            send_sem=send_sem.at[step],
            recv_sem=recv_sem.at[step],
            device_id={"recv": other_recv, "tm": other_tm},
            device_id_type=MESH,
        )

    pl.semaphore_wait(barrier, devices - 1)

    def send_first(step, carry):
        first_copy(step).start()
        return carry

    lax.fori_loop(1, devices, send_first, 0)
    arrived[my_tm, bins_of(my_recv), :] = outgoing[bins_of(me), :]

    cross[...] = jnp.zeros_like(cross)
    place_in = lax.broadcasted_iota(jnp.int32, (lanes, lanes), 0)
    place_out = lax.broadcasted_iota(jnp.int32, (lanes, lanes), 1)
    same_bin = lax.rem(place_in, BINS) == lax.rem(place_out, BINS)

    def stage(turn, carry):
        def wait_first(step, inner):
            first_arrival(step).wait_recv()
            return inner

        lax.fori_loop(jnp.maximum(turn * n_recv, 1), (turn + 1) * n_recv, wait_first, 0)
        group_tm = lax.rem(my_tm - turn + n_tm, n_tm)
        turned = jnp.transpose(arrived[group_tm].astype(f32))
        plain[...] = turned
        turned = turned.astype(bf16)
        for block in range(STEPS):
            owned = (place_in // BINS == owners_ref[block]) & same_bin
            sources[block] = dot(turned, owned.astype(f32).astype(bf16))
        for block in range(STEPS):

            def window(w, sums):
                first = pl.multiple_of(w * width, width)
                x_real = plain[pl.ds(first, width), :]
                x_imag = plain[pl.ds(first + rows, width), :]
                s_real = sources[block, pl.ds(first, width), :]
                s_imag = sources[block, pl.ds(first + rows, width), :]
                out = []
                for slot in range(width):
                    a_real = s_real[slot : slot + 1, :]
                    a_imag = s_imag[slot : slot + 1, :]
                    out.append(sums[2 * slot] + a_real * x_real + a_imag * x_imag)
                    out.append(sums[2 * slot + 1] + a_real * x_imag - a_imag * x_real)
                return tuple(out)

            zero = jnp.zeros((width, lanes), f32)
            sums = lax.fori_loop(0, windows, window, (zero,) * (2 * width), unroll=2)
            for slot in range(width):
                for part in range(2):
                    first = ((block * 2 + part) * width + slot) * width
                    cross[first : first + width, :] += sums[2 * slot + part]
        return carry

    lax.fori_loop(0, n_tm, stage, 0)

    by_bin = jnp.transpose(cross[...])
    tile = 2 * width * width
    lane = lax.broadcasted_iota(jnp.int32, (PAIRS, tile), 1)
    row = lax.broadcasted_iota(jnp.int32, (PAIRS, tile), 0)
    is_real = lane < width * width
    lone = (row + me) == 0
    for recv in range(n_recv):
        for tm in range(n_tm):
            column = slice(tm * tile, (tm + 1) * tile)
            bottom = by_bin[recv * BINS : recv * BINS + PAIRS, column]
            mirror = by_bin[recv * BINS + PAIRS : (recv + 1) * BINS, column]
            pair = jnp.where(is_real, bottom + mirror, bottom - mirror)
            alone = jnp.where(is_real, bottom, pltpu.roll(mirror, width * width, 1))
            first = (recv * n_tm + tm) * PAIRS
            folded[first : first + PAIRS, :] = jnp.where(lone, alone, pair)

    def pairs_of(device):
        return pl.ds(pl.multiple_of(device * PAIRS, PAIRS), PAIRS)

    def second_copy(step, sign):
        other_recv, other_tm = partner(step, sign)
        other = other_recv * n_tm + other_tm
        return pltpu.make_async_remote_copy(
            src_ref=folded.at[pairs_of(other)],
            dst_ref=landed.at[pairs_of(me if sign > 0 else other)],
            send_sem=send2_sem.at[step],
            recv_sem=recv2_sem.at[step],
            device_id={"recv": other_recv, "tm": other_tm},
            device_id_type=MESH,
        )

    def send_second(step, carry):
        second_copy(step, 1).start()
        return carry

    lax.fori_loop(1, devices, send_second, 0)
    landed[pairs_of(me), :] = folded[pairs_of(me), :]

    to = lax.broadcasted_iota(jnp.int32, (tile, tile), 0)
    frm = lax.broadcasted_iota(jnp.int32, (tile, tile), 1)
    to_slot = lax.rem(to // width, width)
    wanted = jnp.zeros_like(to)
    for j in range(width):
        wanted = jnp.where(to_slot == j, slots_ref[my_tm, j], wanted)
    picks = (
        (to // (width * width) == frm // (width * width))
        & (lax.rem(to, width) == lax.rem(frm, width))
        & (lax.rem(frm // width, width) == wanted)
    ).astype(f32).astype(bf16)

    def wait_second(step, carry):
        second_copy(step, -1).wait_recv()
        return carry

    lax.fori_loop(1, devices, wait_second, 0)

    square = width * width
    flat_high, flat_rest = [
        jnp.concatenate([picked[:square], picked[square:]], axis=1).astype(bf16)
        for picked in (dot(picks, half) for half in split(jnp.transpose(landed[...])))
    ]
    high = high_ref[...]
    lags = dot(flat_high, high) + (dot(flat_rest, high) + dot(flat_high, rest_ref[...]))
    out_ref[...] = lags.reshape(width, width, length)

    def wait_sent(step, carry):
        first_copy(step).wait_send()
        second_copy(step, 1).wait_send()
        return carry

    lax.fori_loop(1, devices, wait_sent, 0)


def per_device_split(n_recv, n_tm, spectra, owners, source_slots):
    _, windows, width, length = spectra.shape
    devices = n_recv * n_tm
    lanes = n_recv * BINS
    tile = 2 * width * width
    rows = windows * width
    vmem = pl.BlockSpec(memory_space=pltpu.VMEM)
    smem = pl.BlockSpec(memory_space=pltpu.SMEM)

    def body(*refs):
        kernel(n_recv, n_tm, windows, width, length, *refs)

    return pl.pallas_call(
        body,
        out_shape=jax.ShapeDtypeStruct((width, width, length), jnp.float32),
        in_specs=[vmem, smem, smem, vmem, vmem, vmem, vmem, vmem],
        out_specs=vmem,
        scratch_shapes=[
            pltpu.VMEM((length, 2 * rows), jnp.bfloat16),
            pltpu.VMEM((n_tm, lanes, 2 * rows), jnp.bfloat16),
            pltpu.VMEM((2 * rows, lanes), jnp.float32),
            pltpu.VMEM((STEPS, 2 * rows, lanes), jnp.float32),
            pltpu.VMEM((STEPS * tile, lanes), jnp.float32),
            pltpu.VMEM((devices * PAIRS, tile), jnp.float32),
            pltpu.VMEM((devices * PAIRS, tile), jnp.float32),
            pltpu.SemaphoreType.DMA((devices,)),
            pltpu.SemaphoreType.DMA((devices,)),
            pltpu.SemaphoreType.DMA((devices,)),
            pltpu.SemaphoreType.DMA((devices,)),
        ],
        compiler_params=pltpu.CompilerParams(
            collective_id=0, has_side_effects=True, vmem_limit_bytes=32 * 1024 * 1024
        ),
        name="whiten_exchange_correlate",
    )(spectra, owners, source_slots, *(jnp.asarray(t) for t in constant_tables(length)))


def solution(mesh):
    n_recv, n_tm = mesh.shape["recv"], mesh.shape["tm"]

    def per_device(spectra, owners, source_slots):
        _, _, width, length = spectra.shape
        slots = source_slots.shape[1]
        if n_recv * n_tm * BINS == length and n_tm == STEPS and slots == width:
            return per_device_split(n_recv, n_tm, spectra, owners, source_slots)
        return per_device_gathered(spectra, owners, source_slots)

    in_specs = (P(None, "tm", "recv", None), P(), P())
    out_specs = P("tm", "recv", None)
    return jax.shard_map(
        per_device, mesh=mesh, in_specs=in_specs, out_specs=out_specs, check_vma=False
    )
```

```python
import math

import jax
import jax.numpy as jnp
import numpy as np
from jax import lax
from jax.experimental import pallas as pl
from jax.experimental.pallas import tpu as pltpu
from jax.sharding import PartitionSpec as P

HALF = 64
STEPS = 4
BINS = 16
PAIRS = BINS // 2

epsilon = 1e-05
MESH = pl.DeviceIdType.MESH
NT = (((1,), (1,)), ((), ()))


def broadcast(value, axis, source):
    kept = jnp.where(lax.axis_index(axis) == source, value, 0).astype(value.dtype)
    return lax.psum(kept, axis)


def band_matrix(length, half_width):
    positions = lax.iota(jnp.int32, length)
    near = (jnp.abs(positions[:, None] - positions[None, :]) <= half_width).astype(jnp.float32)
    return near / jnp.sum(near, axis=0, keepdims=True)


def transform_tables(length):
    positions = lax.iota(jnp.int32, length)
    phase = positions[:, None] * positions[None, :] % length
    angle = phase.astype(jnp.float32) * (2.0 * math.pi / length)
    return (jnp.cos(angle), jnp.sin(angle))


def inverse_lags(cross_real, cross_imag, cosine, sine):
    length = cross_real.shape[-1]
    high = lax.Precision.HIGHEST
    flat_real = cross_real.reshape(-1, length)
    flat_imag = cross_imag.reshape(-1, length)
    lag_terms = jnp.dot(
        flat_real, cosine, precision=high, preferred_element_type=jnp.float32
    ) - jnp.dot(flat_imag, sine, precision=high, preferred_element_type=jnp.float32)
    return (lag_terms / length).reshape(cross_real.shape)


def per_device_gathered(spectra, owners, source_slots):
    length = spectra.shape[3]
    width = spectra.shape[2]
    band_table = band_matrix(length, HALF)
    parts = spectra.astype(jnp.float32)
    energy = parts[0] * parts[0] + parts[1] * parts[1]
    smooth = jnp.dot(
        energy.reshape(-1, length),
        band_table,
        precision=lax.Precision.HIGHEST,
        preferred_element_type=jnp.float32,
    ).reshape(energy.shape)
    whitened = (parts * lax.rsqrt(smooth + epsilon)[None]).astype(jnp.bfloat16)
    positions = lax.iota(jnp.int32, width)
    real_parts = []
    imag_parts = []
    for step in range(STEPS):
        selector = (source_slots[step][:, None] == positions[None, :]).astype(jnp.bfloat16)
        picked = jnp.einsum(
            "sr,cwrf->cwsf", selector, whitened, preferred_element_type=jnp.float32
        ).astype(jnp.bfloat16)
        arrived = broadcast(picked, "recv", owners[step])
        real_parts.append(
            jnp.einsum("wsf,wrf->srf", arrived[0], whitened[0], preferred_element_type=jnp.float32)
            + jnp.einsum(
                "wsf,wrf->srf", arrived[1], whitened[1], preferred_element_type=jnp.float32
            )
        )
        imag_parts.append(
            jnp.einsum("wsf,wrf->srf", arrived[0], whitened[1], preferred_element_type=jnp.float32)
            - jnp.einsum(
                "wsf,wrf->srf", arrived[1], whitened[0], preferred_element_type=jnp.float32
            )
        )
    cross_real = jnp.concatenate(real_parts, axis=0)
    cross_imag = jnp.concatenate(imag_parts, axis=0)
    cosine, sine = transform_tables(length)
    return lax.psum_scatter(
        inverse_lags(cross_real, cross_imag, cosine, sine), "tm", scatter_dimension=0, tiled=True
    )


def folded_table(length):
    low = np.arange(length // 2)
    places = np.arange(length)
    angle = (low[:, None] * places[None, :] % length) * (2.0 * math.pi / length)
    cosine = np.cos(angle) / length
    sine = -np.sin(angle) / length
    sine[0] = np.where(places % 2 == 0, 1.0, -1.0) / length
    return np.concatenate([cosine, sine], axis=0).astype(np.float32)


def split(value):
    high = value.astype(jnp.bfloat16)
    return high, (value - high.astype(jnp.float32)).astype(jnp.bfloat16)


def as_ones(mask):
    return mask.astype(jnp.float32).astype(jnp.bfloat16)


def dot(a, b):
    return jnp.dot(a, b, preferred_element_type=jnp.float32)


def kernel(
    n_recv, n_tm, windows, width, length,
    x_hbm, owners_hbm, slots_hbm, table_hbm,
    out_ref,
    x_ref, owners_ref, slots_ref, table_ref, load_sem,
    regroup_ref,
    outgoing, arrived, plain, sources, cross, folded, landed,
    send_sem, recv_sem, send2_sem, recv2_sem,
):
    f32, bf16 = jnp.float32, jnp.bfloat16
    devices = n_recv * n_tm
    rows = windows * width
    lanes = n_recv * BINS
    my_recv, my_tm = lax.axis_index("recv"), lax.axis_index("tm")
    me = my_tm * n_recv + my_recv

    places = (
        (x_hbm, x_ref), (owners_hbm, owners_ref), (slots_hbm, slots_ref), (table_hbm, table_ref),
    )
    loads = [
        pltpu.make_async_copy(source, target, load_sem.at[number])
        for number, (source, target) in enumerate(places)
    ]
    for load in loads:
        load.start()

    def partner(step, sign):
        other_recv = lax.rem(my_recv + sign * lax.rem(step, n_recv) + n_recv, n_recv)
        other_tm = lax.rem(my_tm + sign * (step // n_recv) + n_tm, n_tm)
        return other_recv, other_tm

    barrier = pltpu.get_barrier_semaphore()

    def greet(step, carry):
        other_recv, other_tm = partner(step, 1)
        pl.semaphore_signal(
            barrier, inc=1, device_id={"recv": other_recv, "tm": other_tm}, device_id_type=MESH
        )
        return carry

    lax.fori_loop(1, devices, greet, 0)

    position = lax.broadcasted_iota(jnp.int32, (1, length), 1)
    count = jnp.minimum(position, HALF) + jnp.minimum(length - 1 - position, HALF) + 1
    share = 1.0 / count.astype(f32)
    row = lax.broadcasted_iota(jnp.int32, (length, length), 0)
    column = lax.broadcasted_iota(jnp.int32, (length, length), 1)
    near = as_ones(jnp.abs(row - column) <= HALF)
    low = row // BINS * PAIRS + lax.rem(row, PAIRS)
    mirror = jnp.where(low == 0, length // 2, length - low)
    regroup_ref[...] = as_ones(jnp.where(lax.rem(row, BINS) < PAIRS, low, mirror) == column)
    loads[0].wait()
    real = x_ref[0].astype(f32).reshape(rows, length)
    imag = x_ref[1].astype(f32).reshape(rows, length)
    energy_high, energy_rest = split(real * real + imag * imag)
    smooth = (dot(energy_high, near) + dot(energy_rest, near)) * share
    gain = lax.rsqrt(smooth + epsilon)
    white = jnp.concatenate([real * gain, imag * gain], axis=0).astype(bf16)

    def bins_of(device):
        return pl.ds(pl.multiple_of(device * BINS, BINS), BINS)

    def first_copy(step):
        other_recv, other_tm = partner(step, 1)
        return pltpu.make_async_remote_copy(
            src_ref=outgoing.at[bins_of(other_tm * n_recv + other_recv)],
            dst_ref=arrived.at[my_tm, bins_of(my_recv)],
            send_sem=send_sem.at[step],
            recv_sem=recv_sem.at[step],
            device_id={"recv": other_recv, "tm": other_tm},
            device_id_type=MESH,
        )

    def first_arrival(step):
        other_recv, other_tm = partner(step, -1)
        return pltpu.make_async_remote_copy(
            src_ref=outgoing.at[bins_of(other_tm * n_recv + other_recv)],
            dst_ref=arrived.at[other_tm, bins_of(other_recv)],
            send_sem=send_sem.at[step],
            recv_sem=recv_sem.at[step],
            device_id={"recv": other_recv, "tm": other_tm},
            device_id_type=MESH,
        )

    pl.semaphore_wait(barrier, devices - 1)

    def send_first(step, carry):
        first_copy(step).start()
        return carry

    for turn in range(n_tm):
        group = pl.ds(pl.multiple_of(lax.rem(my_tm + turn, n_tm) * lanes, lanes), lanes)
        outgoing[group, :] = lax.dot_general(
            regroup_ref[group, :], white, NT, preferred_element_type=f32
        ).astype(bf16)
        lax.fori_loop(max(turn * n_recv, 1), (turn + 1) * n_recv, send_first, 0)
    arrived[my_tm, bins_of(my_recv), :] = outgoing[bins_of(me), :]

    cross[...] = jnp.zeros_like(cross)
    for load in loads[1:]:
        load.wait()
    place_in = lax.broadcasted_iota(jnp.int32, (lanes, lanes), 0)
    place_out = lax.broadcasted_iota(jnp.int32, (lanes, lanes), 1)
    same_bin = lax.rem(place_in, BINS) == lax.rem(place_out, BINS)

    def stage(turn, carry):
        def wait_first(step, inner):
            first_arrival(step).wait_recv()
            return inner

        lax.fori_loop(jnp.maximum(turn * n_recv, 1), (turn + 1) * n_recv, wait_first, 0)
        group_tm = lax.rem(my_tm - turn + n_tm, n_tm)
        turned = jnp.transpose(arrived[group_tm].astype(f32))
        plain[...] = turned
        turned = turned.astype(bf16)
        for block in range(STEPS):
            owned = (place_in // BINS == owners_ref[block]) & same_bin
            sources[block] = dot(turned, as_ones(owned))
        for block in range(STEPS):

            def window(w, sums):
                first = pl.multiple_of(w * width, width)
                x_real = plain[pl.ds(first, width), :]
                x_imag = plain[pl.ds(first + rows, width), :]
                s_real = sources[block, pl.ds(first, width), :]
                s_imag = sources[block, pl.ds(first + rows, width), :]
                out = []
                for slot in range(width):
                    a_real = s_real[slot : slot + 1, :]
                    a_imag = s_imag[slot : slot + 1, :]
                    out.append(sums[2 * slot] + a_real * x_real + a_imag * x_imag)
                    out.append(sums[2 * slot + 1] + a_real * x_imag - a_imag * x_real)
                return tuple(out)

            zero = jnp.zeros((width, lanes), f32)
            sums = lax.fori_loop(0, windows, window, (zero,) * (2 * width), unroll=2)
            for slot in range(width):
                for part in range(2):
                    first = ((block * 2 + part) * width + slot) * width
                    cross[first : first + width, :] += sums[2 * slot + part]
        return carry

    lax.fori_loop(0, n_tm, stage, 0)

    by_bin = jnp.transpose(cross[...])
    tile = 2 * width * width
    lane = lax.broadcasted_iota(jnp.int32, (PAIRS, tile), 1)
    row = lax.broadcasted_iota(jnp.int32, (PAIRS, tile), 0)
    is_real = lane < width * width
    lone = (row + me) == 0
    for recv in range(n_recv):
        for tm in range(n_tm):
            column = slice(tm * tile, (tm + 1) * tile)
            bottom = by_bin[recv * BINS : recv * BINS + PAIRS, column]
            mirror = by_bin[recv * BINS + PAIRS : (recv + 1) * BINS, column]
            pair = jnp.where(is_real, bottom + mirror, bottom - mirror)
            alone = jnp.where(is_real, bottom, pltpu.roll(mirror, width * width, 1))
            first = (tm * n_recv + recv) * PAIRS
            folded[first : first + PAIRS, :] = jnp.where(lone, alone, pair)

    def pairs_of(device):
        return pl.ds(pl.multiple_of(device * PAIRS, PAIRS), PAIRS)

    def second_copy(step, sign):
        other_recv, other_tm = partner(step, sign)
        other = other_tm * n_recv + other_recv
        return pltpu.make_async_remote_copy(
            src_ref=folded.at[pairs_of(other)],
            dst_ref=landed.at[pairs_of(me if sign > 0 else other)],
            send_sem=send2_sem.at[step],
            recv_sem=recv2_sem.at[step],
            device_id={"recv": other_recv, "tm": other_tm},
            device_id_type=MESH,
        )

    def send_second(step, carry):
        second_copy(step, 1).start()
        return carry

    lax.fori_loop(1, devices, send_second, 0)
    landed[pairs_of(me), :] = folded[pairs_of(me), :]

    to = lax.broadcasted_iota(jnp.int32, (tile, tile), 0)
    frm = lax.broadcasted_iota(jnp.int32, (tile, tile), 1)
    to_slot = lax.rem(to // width, width)
    wanted = jnp.zeros_like(to)
    for j in range(width):
        wanted = jnp.where(to_slot == j, slots_ref[my_tm, j], wanted)
    picks = as_ones(
        (to // (width * width) == frm // (width * width))
        & (lax.rem(to, width) == lax.rem(frm, width))
        & (lax.rem(frm // width, width) == wanted)
    )
    high, rest = split(table_ref[...])

    def wait_second(step, carry):
        second_copy(step, -1).wait_recv()
        return carry

    lax.fori_loop(1, devices, wait_second, 0)

    square = width * width
    flat_high, flat_rest = [
        jnp.concatenate([picked[:square], picked[square:]], axis=1).astype(bf16)
        for picked in (dot(picks, half) for half in split(jnp.transpose(landed[...])))
    ]
    lags = dot(flat_high, high) + (dot(flat_rest, high) + dot(flat_high, rest))
    out_ref[...] = lags.reshape(width, width, length)

    def wait_sent(step, carry):
        first_copy(step).wait_send()
        second_copy(step, 1).wait_send()
        return carry

    lax.fori_loop(1, devices, wait_sent, 0)


def per_device_split(n_recv, n_tm, spectra, owners, source_slots):
    _, windows, width, length = spectra.shape
    devices = n_recv * n_tm
    lanes = n_recv * BINS
    tile = 2 * width * width
    rows = windows * width
    vmem = pl.BlockSpec(memory_space=pltpu.VMEM)
    operands = (spectra, owners, source_slots, jnp.asarray(folded_table(length)))
    scalars = (owners, source_slots)
    held = [
        (pltpu.SMEM if any(one is s for s in scalars) else pltpu.VMEM)(one.shape, one.dtype)
        for one in operands
    ]

    def body(*refs):
        kernel(n_recv, n_tm, windows, width, length, *refs)

    return pl.pallas_call(
        body,
        out_shape=jax.ShapeDtypeStruct((width, width, length), jnp.float32),
        in_specs=[pl.BlockSpec(memory_space=pltpu.MemorySpace.HBM)] * len(operands),
        out_specs=vmem,
        scratch_shapes=[
            *held,
            pltpu.SemaphoreType.DMA((len(operands),)),
            pltpu.VMEM((length, length), jnp.bfloat16),
            pltpu.VMEM((length, 2 * rows), jnp.bfloat16),
            pltpu.VMEM((n_tm, lanes, 2 * rows), jnp.bfloat16),
            pltpu.VMEM((2 * rows, lanes), jnp.float32),
            pltpu.VMEM((STEPS, 2 * rows, lanes), jnp.float32),
            pltpu.VMEM((STEPS * tile, lanes), jnp.float32),
            pltpu.VMEM((devices * PAIRS, tile), jnp.float32),
            pltpu.VMEM((devices * PAIRS, tile), jnp.float32),
            pltpu.SemaphoreType.DMA((devices,)),
            pltpu.SemaphoreType.DMA((devices,)),
            pltpu.SemaphoreType.DMA((devices,)),
            pltpu.SemaphoreType.DMA((devices,)),
        ],
        compiler_params=pltpu.CompilerParams(collective_id=0, has_side_effects=True),
        name="whiten_exchange_correlate",
    )(*operands)


def solution(mesh):
    n_recv, n_tm = mesh.shape["recv"], mesh.shape["tm"]

    def per_device(spectra, owners, source_slots):
        _, _, width, length = spectra.shape
        slots = source_slots.shape[1]
        if n_recv * n_tm * BINS == length and n_tm == STEPS and slots == width:
            return per_device_split(n_recv, n_tm, spectra, owners, source_slots)
        return per_device_gathered(spectra, owners, source_slots)

    in_specs = (P(None, "tm", "recv", None), P(), P())
    out_specs = P("tm", "recv", None)
    return jax.shard_map(
        per_device, mesh=mesh, in_specs=in_specs, out_specs=out_specs, check_vma=False
    )
```

```python
import math

import jax
import jax.numpy as jnp
import numpy as np
from jax import lax
from jax.experimental import pallas as pl
from jax.experimental.pallas import tpu as pltpu
from jax.sharding import PartitionSpec as P

HALF = 64
LANES = 128
STEPS = 4
BINS = 16
PAIRS = BINS // 2

epsilon = 1e-05
MESH = pl.DeviceIdType.MESH
NT = (((1,), (1,)), ((), ()))


def broadcast(value, axis, source):
    kept = jnp.where(lax.axis_index(axis) == source, value, 0).astype(value.dtype)
    return lax.psum(kept, axis)


def band_matrix(length, half_width):
    positions = lax.iota(jnp.int32, length)
    near = (jnp.abs(positions[:, None] - positions[None, :]) <= half_width).astype(jnp.float32)
    return near / jnp.sum(near, axis=0, keepdims=True)


def transform_tables(length):
    positions = lax.iota(jnp.int32, length)
    phase = positions[:, None] * positions[None, :] % length
    angle = phase.astype(jnp.float32) * (2.0 * math.pi / length)
    return (jnp.cos(angle), jnp.sin(angle))


def inverse_lags(cross_real, cross_imag, cosine, sine):
    length = cross_real.shape[-1]
    high = lax.Precision.HIGHEST
    flat_real = cross_real.reshape(-1, length)
    flat_imag = cross_imag.reshape(-1, length)
    lag_terms = jnp.dot(
        flat_real, cosine, precision=high, preferred_element_type=jnp.float32
    ) - jnp.dot(flat_imag, sine, precision=high, preferred_element_type=jnp.float32)
    return (lag_terms / length).reshape(cross_real.shape)


def per_device_gathered(spectra, owners, source_slots):
    length = spectra.shape[3]
    width = spectra.shape[2]
    band_table = band_matrix(length, HALF)
    parts = spectra.astype(jnp.float32)
    energy = parts[0] * parts[0] + parts[1] * parts[1]
    smooth = jnp.dot(
        energy.reshape(-1, length),
        band_table,
        precision=lax.Precision.HIGHEST,
        preferred_element_type=jnp.float32,
    ).reshape(energy.shape)
    whitened = (parts * lax.rsqrt(smooth + epsilon)[None]).astype(jnp.bfloat16)
    positions = lax.iota(jnp.int32, width)
    real_parts = []
    imag_parts = []
    for step in range(STEPS):
        selector = (source_slots[step][:, None] == positions[None, :]).astype(jnp.bfloat16)
        picked = jnp.einsum(
            "sr,cwrf->cwsf", selector, whitened, preferred_element_type=jnp.float32
        ).astype(jnp.bfloat16)
        arrived = broadcast(picked, "recv", owners[step])
        real_parts.append(
            jnp.einsum("wsf,wrf->srf", arrived[0], whitened[0], preferred_element_type=jnp.float32)
            + jnp.einsum(
                "wsf,wrf->srf", arrived[1], whitened[1], preferred_element_type=jnp.float32
            )
        )
        imag_parts.append(
            jnp.einsum("wsf,wrf->srf", arrived[0], whitened[1], preferred_element_type=jnp.float32)
            - jnp.einsum(
                "wsf,wrf->srf", arrived[1], whitened[0], preferred_element_type=jnp.float32
            )
        )
    cross_real = jnp.concatenate(real_parts, axis=0)
    cross_imag = jnp.concatenate(imag_parts, axis=0)
    cosine, sine = transform_tables(length)
    return lax.psum_scatter(
        inverse_lags(cross_real, cross_imag, cosine, sine), "tm", scatter_dimension=0, tiled=True
    )


def folded_table(length):
    low = np.arange(length // 2)
    places = np.arange(length)
    angle = (low[:, None] * places[None, :] % length) * (2.0 * math.pi / length)
    cosine = np.cos(angle) / length
    sine = -np.sin(angle) / length
    sine[0] = np.where(places % 2 == 0, 1.0, -1.0) / length
    return np.concatenate([cosine, sine], axis=0).astype(np.float32)


def split(value):
    high = value.astype(jnp.bfloat16)
    return high, (value - high.astype(jnp.float32)).astype(jnp.bfloat16)


def as_ones(mask):
    return mask.astype(jnp.float32).astype(jnp.bfloat16)


def dot(a, b):
    return jnp.dot(a, b, preferred_element_type=jnp.float32)


def kernel(
    n_recv, n_tm, windows, width, length,
    x_hbm, owners_hbm, slots_hbm, table_hbm,
    out_ref,
    x_ref, owners_ref, slots_ref, table_ref, load_sem,
    regroup_ref, white_ref, outgoing, arrived, picked, source, receiver, cross, folded, landed,
    send_sem, recv_sem, send2_sem, recv2_sem,
):
    f32, bf16 = jnp.float32, jnp.bfloat16
    devices = n_recv * n_tm
    rows = windows * width
    terms = 2 * windows
    lanes = n_recv * BINS
    my_recv, my_tm = lax.axis_index("recv"), lax.axis_index("tm")
    me = my_tm * n_recv + my_recv

    places = (
        (x_hbm, x_ref), (owners_hbm, owners_ref), (slots_hbm, slots_ref), (table_hbm, table_ref),
    )
    loads = [
        pltpu.make_async_copy(source, target, load_sem.at[number])
        for number, (source, target) in enumerate(places)
    ]
    for load in loads:
        load.start()

    def partner(step, sign):
        other_recv = lax.rem(my_recv + sign * lax.rem(step, n_recv) + n_recv, n_recv)
        other_tm = lax.rem(my_tm + sign * (step // n_recv) + n_tm, n_tm)
        return other_recv, other_tm

    barrier = pltpu.get_barrier_semaphore()

    def greet(step, carry):
        other_recv, other_tm = partner(step, 1)
        pl.semaphore_signal(
            barrier, inc=1, device_id={"recv": other_recv, "tm": other_tm}, device_id_type=MESH
        )
        return carry

    lax.fori_loop(1, devices, greet, 0)

    position = lax.broadcasted_iota(jnp.int32, (1, length), 1)
    count = jnp.minimum(position, HALF) + jnp.minimum(length - 1 - position, HALF) + 1
    share = 1.0 / count.astype(f32)
    row = lax.broadcasted_iota(jnp.int32, (length, length), 0)
    column = lax.broadcasted_iota(jnp.int32, (length, length), 1)
    near = as_ones(jnp.abs(row - column) <= HALF)
    low = row // BINS * PAIRS + lax.rem(row, PAIRS)
    mirror = jnp.where(low == 0, length // 2, length - low)
    regroup_ref[...] = as_ones(jnp.where(lax.rem(row, BINS) < PAIRS, low, mirror) == column)
    loads[0].wait()
    real = x_ref[0].astype(f32).reshape(rows, length)
    imag = x_ref[1].astype(f32).reshape(rows, length)
    energy_high, energy_rest = split(real * real + imag * imag)
    smooth = (dot(energy_high, near) + dot(energy_rest, near)) * share
    gain = lax.rsqrt(smooth + epsilon)
    for part, value in enumerate((real, imag)):
        scaled = value * gain
        for tile in range(length // LANES):
            white_ref[tile, part * rows : (part + 1) * rows, :] = scaled[
                :, tile * LANES : (tile + 1) * LANES
            ]
    white = jnp.concatenate(
        [
            jnp.concatenate(
                [white_ref[tile, pl.ds(c, terms, stride=width), :] for c in range(width)], axis=0
            ).astype(bf16)
            for tile in range(length // LANES)
        ],
        axis=1,
    )

    def bins_of(device):
        return pl.ds(pl.multiple_of(device * BINS, BINS), BINS)

    def first_copy(step):
        other_recv, other_tm = partner(step, 1)
        return pltpu.make_async_remote_copy(
            src_ref=outgoing.at[bins_of(other_tm * n_recv + other_recv)],
            dst_ref=arrived.at[my_tm, bins_of(my_recv)],
            send_sem=send_sem.at[step],
            recv_sem=recv_sem.at[step],
            device_id={"recv": other_recv, "tm": other_tm},
            device_id_type=MESH,
        )

    def first_arrival(step):
        other_recv, other_tm = partner(step, -1)
        return pltpu.make_async_remote_copy(
            src_ref=outgoing.at[bins_of(other_tm * n_recv + other_recv)],
            dst_ref=arrived.at[other_tm, bins_of(other_recv)],
            send_sem=send_sem.at[step],
            recv_sem=recv_sem.at[step],
            device_id={"recv": other_recv, "tm": other_tm},
            device_id_type=MESH,
        )

    pl.semaphore_wait(barrier, devices - 1)

    def send_first(step, carry):
        first_copy(step).start()
        return carry

    for turn in range(n_tm):
        group = pl.ds(pl.multiple_of(lax.rem(my_tm + turn, n_tm) * lanes, lanes), lanes)
        outgoing[group, :] = lax.dot_general(
            regroup_ref[group, :], white, NT, preferred_element_type=f32
        ).astype(bf16)
        lax.fori_loop(max(turn * n_recv, 1), (turn + 1) * n_recv, send_first, 0)
    arrived[my_tm, bins_of(my_recv), :] = outgoing[bins_of(me), :]

    for load in loads[1:]:
        load.wait()

    place = lax.broadcasted_iota(jnp.int32, (STEPS * BINS, lanes), 0)
    origin = lax.broadcasted_iota(jnp.int32, (STEPS * BINS, lanes), 1)
    owner = jnp.zeros_like(place)
    for block in range(STEPS):
        owner = jnp.where(place // BINS == block, owners_ref[block], owner)
    owned = as_ones((origin // BINS == owner) & (lax.rem(origin, BINS) == lax.rem(place, BINS)))

    def wait_first(step, carry):
        first_arrival(step).wait_recv()
        return carry

    for turn in range(n_tm):
        lax.fori_loop(max(turn * n_recv, 1), (turn + 1) * n_recv, wait_first, 0)
        block_in = arrived[lax.rem(my_tm - turn + n_tm, n_tm)]
        turned = jnp.transpose(block_in.astype(f32)).astype(bf16)
        for c in range(width):
            receiver[turn * terms : (turn + 1) * terms, c * lanes : (c + 1) * lanes] = turned[
                c * terms : (c + 1) * terms
            ]
        picked[turn] = dot(owned, block_in)
        if (turn + 1) * terms % LANES == 0:
            group = LANES // terms
            tile = turn // group
            for c in range(width):
                source[tile, pl.ds(c, STEPS * BINS, stride=width), :] = jnp.concatenate(
                    [
                        picked[tile * group + member, :, c * terms : (c + 1) * terms]
                        for member in range(group)
                    ],
                    axis=1,
                )

    depth = n_tm * terms
    term_in = lax.broadcasted_iota(jnp.int32, (depth, depth), 0)
    term_out = lax.broadcasted_iota(jnp.int32, (depth, depth), 1)
    is_first = lax.rem(term_out, terms) < windows
    swap = as_ones((term_in == term_out - windows) & ~is_first) - as_ones(
        (term_in == term_out + windows) & is_first
    )

    tile = 2 * width * width
    lane = lax.broadcasted_iota(jnp.int32, (PAIRS, tile), 1)
    row = lax.broadcasted_iota(jnp.int32, (PAIRS, tile), 0)
    is_real = lane < width * width
    lone = (row + me) == 0
    bin_of = lax.rem(lax.broadcasted_iota(jnp.int32, (width, width * lanes), 1), BINS)

    def pairs_of(device):
        return pl.ds(pl.multiple_of(device * PAIRS, PAIRS), PAIRS)

    def second_copy(step, sign):
        other_recv, other_tm = partner(step, sign)
        other = other_tm * n_recv + other_recv
        return pltpu.make_async_remote_copy(
            src_ref=folded.at[pairs_of(other)],
            dst_ref=landed.at[pairs_of(me if sign > 0 else other)],
            send_sem=send2_sem.at[step],
            recv_sem=recv2_sem.at[step],
            device_id={"recv": other_recv, "tm": other_tm},
            device_id_type=MESH,
        )

    def send_second(step, carry):
        second_copy(step, 1).start()
        return carry

    arrivals = receiver[...]
    block_rows = BINS * width
    for turn in range(n_tm):
        block = lax.rem(my_tm + turn, n_tm)
        chosen = pl.ds(pl.multiple_of(block * block_rows, block_rows), block_rows)
        direct = jnp.concatenate(
            [source[number, chosen, :] for number in range(depth // LANES)], axis=1
        ).astype(bf16)
        swapped = dot(direct, swap).astype(bf16)
        for part, left in enumerate((direct, swapped)):
            products = dot(left, arrivals)
            sums = products[:width]
            for number in range(1, BINS):
                sums = jnp.where(
                    bin_of == number, products[number * width : (number + 1) * width], sums
                )
            for c in range(width):
                first = (part * width + c) * width
                cross[first : first + width, :] = sums[:, c * lanes : (c + 1) * lanes]
        by_bin = jnp.transpose(cross[...])
        for recv in range(n_recv):
            bottom = by_bin[recv * BINS : recv * BINS + PAIRS]
            mirror = by_bin[recv * BINS + PAIRS : (recv + 1) * BINS]
            pair = jnp.where(is_real, bottom + mirror, bottom - mirror)
            alone = jnp.where(is_real, bottom, pltpu.roll(mirror, width * width, 1))
            folded[pairs_of(block * n_recv + recv), :] = jnp.where(lone, alone, pair)
        lax.fori_loop(max(turn * n_recv, 1), (turn + 1) * n_recv, send_second, 0)
    landed[pairs_of(me), :] = folded[pairs_of(me), :]

    to = lax.broadcasted_iota(jnp.int32, (tile, tile), 0)
    frm = lax.broadcasted_iota(jnp.int32, (tile, tile), 1)
    to_slot = lax.rem(to // width, width)
    wanted = jnp.zeros_like(to)
    for j in range(width):
        wanted = jnp.where(to_slot == j, slots_ref[my_tm, j], wanted)
    picks = as_ones(
        (to // (width * width) == frm // (width * width))
        & (lax.rem(to, width) == lax.rem(frm // width, width))
        & (lax.rem(frm, width) == wanted)
    )
    high, rest = split(table_ref[...])

    def wait_second(step, carry):
        second_copy(step, -1).wait_recv()
        return carry

    lax.fori_loop(1, devices, wait_second, 0)

    square = width * width
    flat_high, flat_rest = [
        jnp.concatenate([picked[:square], picked[square:]], axis=1).astype(bf16)
        for picked in (dot(picks, half) for half in split(jnp.transpose(landed[...])))
    ]
    lags = dot(flat_high, high) + (dot(flat_rest, high) + dot(flat_high, rest))
    out_ref[...] = lags.reshape(width, width, length)

    def wait_sent(step, carry):
        first_copy(step).wait_send()
        second_copy(step, 1).wait_send()
        return carry

    lax.fori_loop(1, devices, wait_sent, 0)


def per_device_split(n_recv, n_tm, spectra, owners, source_slots):
    _, windows, width, length = spectra.shape
    devices = n_recv * n_tm
    lanes = n_recv * BINS
    tile = 2 * width * width
    rows = windows * width
    vmem = pl.BlockSpec(memory_space=pltpu.VMEM)
    operands = (spectra, owners, source_slots, jnp.asarray(folded_table(length)))
    scalars = (owners, source_slots)
    held = [
        (pltpu.SMEM if any(one is s for s in scalars) else pltpu.VMEM)(one.shape, one.dtype)
        for one in operands
    ]

    def body(*refs):
        kernel(n_recv, n_tm, windows, width, length, *refs)

    return pl.pallas_call(
        body,
        out_shape=jax.ShapeDtypeStruct((width, width, length), jnp.float32),
        in_specs=[pl.BlockSpec(memory_space=pltpu.MemorySpace.HBM)] * len(operands),
        out_specs=vmem,
        scratch_shapes=[
            *held,
            pltpu.SemaphoreType.DMA((len(operands),)),
            pltpu.VMEM((length, length), jnp.bfloat16),
            pltpu.VMEM((length // LANES, 2 * rows, LANES), jnp.float32),
            pltpu.VMEM((length, 2 * rows), jnp.bfloat16),
            pltpu.VMEM((n_tm, lanes, 2 * rows), jnp.bfloat16),
            pltpu.VMEM((n_tm, STEPS * BINS, 2 * rows), jnp.float32),
            pltpu.VMEM((n_tm * 2 * windows // LANES, STEPS * BINS * width, LANES), jnp.float32),
            pltpu.VMEM((n_tm * 2 * windows, width * lanes), jnp.bfloat16),
            pltpu.VMEM((tile, lanes), jnp.float32),
            pltpu.VMEM((devices * PAIRS, tile), jnp.float32),
            pltpu.VMEM((devices * PAIRS, tile), jnp.float32),
            pltpu.SemaphoreType.DMA((devices,)),
            pltpu.SemaphoreType.DMA((devices,)),
            pltpu.SemaphoreType.DMA((devices,)),
            pltpu.SemaphoreType.DMA((devices,)),
        ],
        compiler_params=pltpu.CompilerParams(collective_id=0, has_side_effects=True),
        name="whiten_exchange_correlate",
    )(*operands)


def solution(mesh):
    n_recv, n_tm = mesh.shape["recv"], mesh.shape["tm"]

    def per_device(spectra, owners, source_slots):
        _, _, width, length = spectra.shape
        slots = source_slots.shape[1]
        if n_recv * n_tm * BINS == length and n_tm == STEPS and slots == width:
            return per_device_split(n_recv, n_tm, spectra, owners, source_slots)
        return per_device_gathered(spectra, owners, source_slots)

    in_specs = (P(None, "tm", "recv", None), P(), P())
    out_specs = P("tm", "recv", None)
    return jax.shard_map(
        per_device, mesh=mesh, in_specs=in_specs, out_specs=out_specs, check_vma=False
    )
```
